512 devices in a mesh: dp: 64 (over z_lo, y, core), tensor: 8 (over x, z_hi).
Axes of the slice: x: 4, y: 4, z: 16 (z_hi: 2, z_lo: 8; z = z_hi * 8 + z_lo), core: 2. Of those that a mesh axis runs over, the one named last changes fastest.
Arguments:
- inputs: bfloat16 [8192, 8192], P('dp'), may hold values from -6 to 6
- weight_blocks: bfloat16 [112, 4096, 128], P('tensor', 'dp'), may hold values from -0.09375 to 0.09375
- block_rows: int32 [112, 32], P('tensor'), may hold values from 0 to 63, as said below
- grad_hidden: bfloat16 [8192, 14336], P('dp', 'tensor'), may hold values from -6 to 6
- projection: bfloat16 [64, 8192], replicated, may hold values from -0.0009765625 to 0.0009765625
- momentum: float32 [64, 14336], P('dp', 'tensor'), may hold values from -6 to 6
Outputs:
- hidden: bfloat16 [8192, 14336], P('dp', 'tensor')
- input_grad: bfloat16 [8192, 8192], P('dp', 'tensor')
- new_momentum: float32 [64, 14336], P('dp', 'tensor')
The draws below stay inside these ranges and needn't reach their ends.
Inputs may be any that keep to these rules, and one draw needn't show every extreme that they name: `block_rows`: the 32 entries of a row are different block rows. Block columns 2j and 2j + 1 together name every block row exactly once.
All inputs are finite; a program needn't handle non-finite values.
Results may differ from the reference program's by a relative error of at most 0.015.
Values may be sent and summed in bfloat16 or wider, within the bound.
No kernel may reach another device: no remote copies, remote signals or barrier semaphores. Data moves between devices by JAX's collectives and lax.ppermute only.
A program may use at most 128 MiB of HBM per device.

```python
import jax
import jax.numpy as jnp
from jax import lax

D = 8192
FF = 14336
BLK = 128
RANK = 64
TOKENS = 8192
PANELS = 112
NZ = 32
N_TENSOR = 8


def draw_block_rows(key, part):
    key = jax.random.fold_in(key, 3)
    rows_total = D // BLK
    pair_keys = jax.random.split(key, PANELS // 2)

    def one_pair(pair_key):
        shuffled = jax.random.permutation(pair_key, jnp.arange(rows_total, dtype=jnp.int32))
        lower_half = jnp.sort(shuffled[:NZ])
        upper_half = jnp.sort(shuffled[NZ:])
        return jnp.stack([lower_half, upper_half])
    paired = jax.vmap(one_pair)(pair_keys)
    return paired.reshape(PANELS, NZ).astype(jnp.int32)


def shard_levels(own_key, shape, cuts, smallest, high):
    factor_of, own = 1.0, jax.random.fold_in(own_key, 6)
    for position, parts in cuts:
        heights = jnp.exp(jax.random.uniform(jax.random.fold_in(own, position), (parts,), jnp.float32, smallest / len(cuts), high / len(cuts)))
        factor_of = factor_of * jnp.repeat(heights, shape[position] // parts).reshape([-1 if axis == position else 1 for axis in range(len(shape))])
    return factor_of


def scatter_about(key, extent, deviation, reach, shards=(), kind=jnp.bfloat16):
    loudness = shard_levels(key, extent, shards, -0.22, 0.18) if shards else 1.0
    array = jax.random.normal(key, extent, jnp.float32) * deviation * loudness
    return jnp.minimum(jnp.maximum(array, -reach), reach).astype(kind)


def setup_inputs(seed: int = 0) -> dict:
    streams_of = jax.random.split(jax.random.key(seed), 7)
    return {
        "inputs": scatter_about(streams_of[0], (TOKENS, D), 1.0, 6.0, ((0, 64),)),
        "weight_blocks": scatter_about(streams_of[1], (PANELS, NZ * BLK, BLK), (NZ * BLK) ** -0.5, 0.09375, ((0, 8), (1, 64))),
        "block_rows": draw_block_rows(jax.random.fold_in(streams_of[6], 71), 0),
        "grad_hidden": scatter_about(streams_of[3], (TOKENS, FF), 1.0, 6.0, ((0, 64), (1, 8))),
        "projection": scatter_about(streams_of[4], (RANK, D), (NZ * BLK * TOKENS) ** -0.5, 0.0009765625),
        "momentum": scatter_about(streams_of[5], (RANK, FF), 1.0, 6.0, ((0, 64), (1, 8)), jnp.float32),
    }


def product(left, right):
    return jnp.dot(left.astype(jnp.float32), right.astype(jnp.float32), precision=lax.Precision.HIGHEST)


def reference(inputs, weight_blocks, block_rows, grad_hidden, projection, momentum):
    per_slice = PANELS // N_TENSOR
    offsets = jnp.arange(BLK, dtype=jnp.int32)

    def panel_step(accumulated, panel_index):
        rows_here = lax.dynamic_index_in_dim(block_rows, panel_index, 0, keepdims=False)
        col_index = (rows_here[:, None] * BLK + offsets[None, :]).reshape(-1).astype(jnp.int32)
        picked = jnp.take(inputs, col_index, axis=1).astype(jnp.float32)
        weights_here = lax.dynamic_index_in_dim(weight_blocks, panel_index, 0, keepdims=False).astype(jnp.float32)
        grads_here = lax.dynamic_slice_in_dim(grad_hidden, panel_index * BLK, BLK, 1).astype(jnp.float32)
        hidden_panel = product(picked, weights_here).astype(jnp.bfloat16)
        contribution = product(grads_here, weights_here.T)
        accumulated = accumulated.at[:, col_index].add(contribution)
        chosen = jnp.take(projection, col_index, axis=1)
        projected = product(chosen, picked.T)
        compressed_panel = product(projected, grads_here)
        return accumulated, (hidden_panel, compressed_panel)

    def slice_step(grand_total, slice_index):
        indices = (slice_index * per_slice + jnp.arange(per_slice, dtype=jnp.int32)).astype(jnp.int32)
        accumulated, outputs = lax.scan(panel_step, jnp.zeros((TOKENS, D), jnp.float32), indices)
        rounded = lax.optimization_barrier(accumulated.astype(jnp.bfloat16)).astype(jnp.float32)
        return grand_total + rounded, outputs

    grand_total, (hidden_parts, compressed_parts) = lax.scan(
        slice_step, jnp.zeros((TOKENS, D), jnp.float32), jnp.arange(N_TENSOR, dtype=jnp.int32))
    hidden = hidden_parts.reshape(PANELS, TOKENS, BLK).transpose(1, 0, 2).reshape(TOKENS, FF)
    compressed = compressed_parts.reshape(PANELS, RANK, BLK).transpose(1, 0, 2).reshape(RANK, FF)
    input_grad = grand_total.astype(jnp.bfloat16)
    new_momentum = 0.9 * momentum + compressed
    return (hidden, input_grad, new_momentum)
```

```python
import functools

import jax
import jax.numpy as jnp
from jax import lax
from jax.experimental import pallas as pl
from jax.experimental.pallas import tpu as pltpu
from jax.sharding import PartitionSpec as P

PARTS = 2
Z, Y, C = 8, 4, 2
X, H = 4, 2
F32, BF16 = jnp.float32, jnp.bfloat16
NT = (((1,), (1,)), ((), ()))


def place(z, y, core):
    return (z * Y + y) * C + core


def every(order):
    return [order(z, y, core) for z in range(Z) for y in range(Y) for core in range(C)]


def flipped(bits):
    return every(lambda z, y, core: (place(z, y, core), place(z ^ (bits // Y), y ^ (bits % Y), core)))


OTHER_CORE = every(lambda z, y, core: (place(z, y, core), place(z, y, 1 - core)))
Z_STEPS = (16, 8, 4)
Y_STEPS = ((1, 3), (3, 1))
X_RINGS = [[x * H + h for x in range(X)] for h in range(H)]
CORNERS = [
    [place(z, y, core) * (X * H) + x * H + h for h in range(H) for core in range(C)]
    for z in range(Z)
    for y in range(Y)
    for x in range(X)
]


def corner(far_h, far_core):
    return [(i, i ^ (far_core * X * H + far_h)) for i in range(Z * Y * C * X * H)]


def after(value, *earlier):
    for e in earlier:
        value = value + jnp.minimum(jnp.abs(e[(0,) * e.ndim]), 0).astype(value.dtype)
    return value


def params(**more):
    return pltpu.CompilerParams(vmem_limit_bytes=50 * 1024 * 1024, **more)


def cost(flops, moved):
    return pl.CostEstimate(flops=flops, bytes_accessed=moved, transcendentals=0)


def regroup(width, parts, half):
    rows = half // parts
    column = lax.broadcasted_iota(jnp.int32, (1, width), 1)
    block, inside = column // (2 * half), column % (2 * half)
    side, deep = inside // half, inside % half
    part, row = deep // rows, deep % rows
    blocks = width // (2 * half)
    source = ((side * parts + part) * blocks + block) * rows + row
    here = lax.broadcasted_iota(jnp.int32, (width, width), 0)
    return jnp.where(here == source, 1.0, 0.0).astype(BF16)


def split_kernel(parts, half, who, x_ref, p_ref, keep_ref, send_ref, proj_ref, order):
    core = who[0]
    width = order.shape[0]
    piece = width // (2 * parts)
    full = keep_ref.shape[1] // parts
    order[...] = regroup(width, parts, half)
    groups = x_ref.shape[1] // width

    def mix(ref):
        stacked = jnp.concatenate([ref[:, g * width : (g + 1) * width] for g in range(groups)], axis=0)
        return lax.dot_general(stacked, order[...], NT, preferred_element_type=F32).astype(BF16)

    x_mixed, p_mixed = mix(x_ref), mix(p_ref)

    def deal(mixed, ref, side):
        rows = ref.shape[0]
        for g in range(groups):
            for p in range(parts):
                to = slice(p * full + g * piece, p * full + (g + 1) * piece)
                at = (side * parts + p) * piece
                ref[:, to] = mixed[g * rows : (g + 1) * rows, at : at + piece]

    for value in range(C):

        @pl.when(core == value)
        def _(value=value):
            deal(x_mixed, keep_ref, value)
            deal(x_mixed, send_ref, 1 - value)
            deal(p_mixed, proj_ref, value)


def compress_kernel(xk_ref, xr_ref, gk_ref, gr_ref, proj_ref, mask_ref, out_ref, masked):
    rank = proj_ref.shape[0]
    pairs = mask_ref.shape[0]
    side = 2 * mask_ref.shape[0]
    block = gk_ref.shape[1] // side
    for j in range(pairs):
        masked[j * rank : (j + 1) * rank, :] = proj_ref[...] * mask_ref[j : j + 1, :]
    masked[pairs * rank : (pairs + 1) * rank, :] = proj_ref[...]
    held = []
    for x_ref in (xk_ref, xr_ref):
        held.append(lax.dot_general(masked[...], x_ref[...], NT, preferred_element_type=F32))
    for panel in range(side):
        total = None
        for seen, g_ref in zip(held, (gk_ref, gr_ref)):
            j = panel // 2
            part = seen[j * rank : (j + 1) * rank, :]
            if panel % 2:
                part = seen[pairs * rank :, :] - part
            high = part.astype(BF16)
            low = (part - high.astype(F32)).astype(BF16)
            grads = g_ref[:, panel * block : (panel + 1) * block]
            term = jnp.dot(high, grads, preferred_element_type=F32) + jnp.dot(low, grads, preferred_element_type=F32)
            total = term if total is None else total + term
        out_ref[:, panel, :] = total


def main_kernel(first, last, who, rows_ref, *rest):
    rest = list(rest)
    chunks = [rest.pop(0) for _ in range(4 if first else 1)]
    xk_ref, xr_ref, gk_ref, gr_ref = (rest.pop(0) for _ in range(4))
    acc_k, acc_r = (None, None) if first else (rest.pop(0), rest.pop(0))
    grad_ref, hk_ref, hr_ref, dense = rest
    core, mine = who[0], who[1]
    deep, block = chunks[0].shape[-2:]
    panels = rows_ref.shape[0]
    some = panels // 2
    tokens = xk_ref.shape[0]
    blank = jnp.zeros((deep, block), BF16)

    def lay(panel, slot, weights):
        at = pl.multiple_of(rows_ref[panel, slot] * deep, deep)
        other = panel ^ 1
        dense[pl.ds(at, deep), panel * block : (panel + 1) * block] = weights
        dense[pl.ds(at, deep), other * block : (other + 1) * block] = blank

    def put(slot, carry):
        for panel in range(panels):
            lay(panel, slot, chunks[0][panel, slot, core])
        return carry

    def put_steps(i, carry):
        for q, (y_first, y_second) in enumerate(Y_STEPS):
            for late in range(2):
                far = (i // 8) * y_first ^ late * y_second
                slot = mine ^ far ^ ((i // 4) % 2 * Z_STEPS[2]) ^ ((i // 2) % 2 * Z_STEPS[1]) ^ (i % 2 * Z_STEPS[0])
                for n in range(some):
                    lay(q * some + n, slot, chunks[2 * q + late][i, n])
        return carry

    if first:
        lax.fori_loop(0, chunks[0].shape[0], put_steps, 0)
    else:
        lax.fori_loop(0, chunks[0].shape[1], put, 0)
    share = dense.shape[0] // (X * H)
    for x in range(X):
        tile = dense[x * H * share : (x + 1) * H * share, :]
        for t, g_ref in enumerate((gk_ref, gr_ref)):
            out = lax.dot_general(g_ref[...], tile, NT, preferred_element_type=F32).astype(BF16)
            for h in range(H):
                grad_ref[x, h, t * tokens : (t + 1) * tokens, :] = out[:, h * share : (h + 1) * share]
    step = 2 * block
    for n in range(panels // 2):
        cols = slice(n * step, (n + 1) * step)
        for x_ref, h_ref, acc in ((xk_ref, hk_ref, acc_k), (xr_ref, hr_ref, acc_r)):
            out = jnp.dot(x_ref[...], dense[:, cols], preferred_element_type=F32)
            if acc is not None:
                out = out + acc[:, cols]
            h_ref[:, cols] = out.astype(h_ref.dtype)


def reduce_kernel(near, who, r_ref, *outs):
    core, h_here = who[0], who[2]
    tokens = outs[0].shape[-2]
    for far_h in range(H):
        for side in range(C):
            at = pl.ds(side * tokens, tokens) if near else pl.ds(pl.multiple_of((side ^ core) * tokens, tokens), tokens)
            h = h_here ^ far_h if near else far_h
            total = r_ref[0, h, at, :].astype(F32)
            for x in range(1, X):
                total = total + r_ref[x, h, at, :].astype(F32)
            if near:
                outs[far_h * C + side][...] = total.astype(BF16)
            else:
                outs[0][far_h * C + side] = total.astype(BF16)


def final_kernel(parts, half, who, *refs):
    near, (r,), out_ref = refs[:4], refs[4:-1], refs[-1]
    width = out_ref.shape[1]
    mine = near[0][...].astype(F32) + near[2][...].astype(F32)
    other = near[1][...].astype(F32) + near[3][...].astype(F32)
    columns = []
    for side in range(C):
        columns.append(jnp.where(who[0] == side, mine, other).astype(BF16))
        columns.append((r[side].astype(F32) + r[C + side].astype(F32)).astype(BF16))
    piece = 128
    group = 2 * parts * piece
    order = regroup(group, parts, half)
    for g in range(width // group):
        together = jnp.concatenate([c[:, g * piece : (g + 1) * piece] for c in columns], axis=1)
        out_ref[:, g * group : (g + 1) * group] = jnp.dot(together, order, preferred_element_type=F32).astype(BF16)


def body(inputs, weight_blocks, block_rows, grad_hidden, projection, momentum):
    tokens, width = inputs.shape
    panels, half, block = weight_blocks.shape
    slots = block_rows.shape[1]
    rank = projection.shape[0]
    row_blocks = width // block
    parts, deep = PARTS, half // PARTS
    units = grad_hidden.shape[1]
    here = lax.axis_index("dp")
    who = jnp.stack([here % C, here // C, lax.axis_index("tensor") % H]).astype(jnp.int32)
    smem = pl.BlockSpec(memory_space=pltpu.SMEM)
    vmem = pl.BlockSpec(memory_space=pltpu.VMEM)
    sds = jax.ShapeDtypeStruct

    keep, send, proj = pl.pallas_call(
        functools.partial(split_kernel, parts, half),
        out_shape=(sds((tokens, width // 2), BF16), sds((tokens, width // 2), BF16), sds((rank, width // 2), BF16)),
        in_specs=[smem, vmem, vmem],
        out_specs=(vmem, vmem, vmem),
        scratch_shapes=[pltpu.VMEM((2 * parts * block, 2 * parts * block), BF16)],
        compiler_params=params(),
        cost_estimate=cost(4 * 10**9, 6 * 10**6),
        name="split",
    )(who, inputs, projection)
    received = lax.ppermute(send, "dp", OTHER_CORE)
    grads_received = lax.ppermute(grad_hidden, "dp", OTHER_CORE)

    named = (block_rows[0::2, :, None] == jnp.arange(row_blocks, dtype=jnp.int32)).any(axis=1)
    mask = jnp.tile(jnp.repeat(named, deep, axis=1), (1, parts)).astype(BF16)
    def compress(first_seen, second_seen):
        out = pl.pallas_call(
            compress_kernel,
            out_shape=sds((rank, panels, block), F32),
            in_specs=[vmem] * 6,
            out_specs=vmem,
            scratch_shapes=[pltpu.VMEM(((panels // 2 + 1) * rank, width // 2), BF16)],
            compiler_params=params(),
            cost_estimate=cost(4 * 10**9, 6 * 10**6),
            name="compress",
        )(keep, received, grad_hidden, grads_received, proj, after(mask, first_seen))
        return out, lax.all_to_all(after(out, second_seen), "dp", 0, 0, tiled=True).sum(axis=0)

    finals, crossings, acc = [], [], ()
    whole = lambda *shape: pl.BlockSpec(shape, lambda i: (0,) * len(shape))
    for p in range(parts):
        own = weight_blocks[:, p * deep : (p + 1) * deep]
        if p == 0:
            chunks, seen = own[None], []
            for step in Z_STEPS:
                if step == Z_STEPS[2]:
                    compressed, summed = compress(*seen)
                    chunks = after(chunks, compressed)
                far = lax.ppermute(chunks, "dp", flipped(step))
                seen.append(far)
                chunks = jnp.concatenate([chunks, far])
            gathered = []
            for q, (y_first, y_second) in enumerate(Y_STEPS):
                some = chunks[:, q * (panels // 2) : (q + 1) * (panels // 2)]
                some = jnp.concatenate([some, lax.ppermute(some, "dp", flipped(y_first))])
                gathered += [some, lax.ppermute(some, "dp", flipped(y_second))]
            shapes = [whole(16, panels // 2, deep, block)] * 4
        else:
            gathered = [lax.all_gather(own, "dp", axis=1, tiled=True).reshape(panels, slots, C, deep, block)]
            shapes = [whole(panels, slots, C, deep, block)]
        turn = after(who, crossed) if p else after(who, summed)
        first, last = p == 0, p == parts - 1
        part_spec = pl.BlockSpec((tokens, row_blocks * deep), lambda i, p=p: (0, p))
        h_types = (F32, BF16 if last else F32)
        share = 8 * deep
        grad, *acc = pl.pallas_call(
            functools.partial(main_kernel, first, last),
            grid=(1,),
            out_shape=(
                sds((X, H, 2 * tokens, share), BF16),
                sds((tokens, units), h_types[0]),
                sds((tokens, units), h_types[1]),
            ),
            in_specs=[smem, smem, *shapes, part_spec, part_spec]
            + [whole(tokens, units)] * (2 if first else 4),
            out_specs=(whole(X, H, 2 * tokens, share), whole(tokens, units), whole(tokens, units)),
            scratch_shapes=[pltpu.VMEM((row_blocks * deep, units), BF16)],
            compiler_params=params(),
            cost_estimate=cost(8 * 10**9 // parts, 8 * 10**6),
            name="main",
        )(turn, block_rows, *gathered, keep, received, grad_hidden, grads_received, *acc)
        crossed = lax.all_to_all(grad, "tensor", 0, 0, tiled=True, axis_index_groups=X_RINGS)
        crossings.append(crossed)
    for p in range(parts):
        near = p == 0
        piece = sds((tokens, share), BF16)
        out = pl.pallas_call(
            functools.partial(reduce_kernel, near),
            out_shape=(piece,) * 4 if near else (sds((H * C, tokens, share), BF16),),
            in_specs=[smem, vmem],
            out_specs=(vmem,) * (4 if near else 1),
            compiler_params=params(),
            cost_estimate=cost(10**6, 10**6),
            name="reduce",
        )(after(who, *finals[1:]) if p else after(who, grad), crossings[p])
        reduced = out[0]
        if near:
            finals = [out[0]] + [lax.ppermute(out[i], ("dp", "tensor"), corner(i // C, i % C)) for i in range(1, 4)]
        else:
            finals.append(lax.all_to_all(reduced, ("dp", "tensor"), 0, 0, tiled=True, axis_index_groups=CORNERS))
    hidden_received = lax.ppermute(acc[1], "dp", OTHER_CORE)
    hidden = (acc[0] + hidden_received.astype(F32)).astype(BF16)
    new_momentum = 0.9 * momentum + summed.reshape(1, units)
    input_grad = pl.pallas_call(
        functools.partial(final_kernel, parts, half),
        out_shape=sds((tokens, width // (X * H)), BF16),
        in_specs=[smem] + [vmem] * 5,
        out_specs=vmem,
        compiler_params=params(),
        cost_estimate=cost(10**8, 10**6),
        name="final",
    )(who, *finals)
    return hidden, input_grad, new_momentum


def solution(mesh):
    placed = (
        P("dp", None),
        P("tensor", "dp", None),
        P("tensor", None),
        P("dp", "tensor"),
        P(),
        P("dp", "tensor"),
    )
    return jax.shard_map(
        body,
        mesh=mesh,
        in_specs=placed,
        out_specs=(P("dp", "tensor"), P("dp", "tensor"), P("dp", "tensor")),
        check_vma=False,
    )
```

```python
import functools

import jax
import jax.numpy as jnp
from jax import lax
from jax.experimental import pallas as pl
from jax.experimental.pallas import tpu as pltpu
from jax.sharding import PartitionSpec as P

PARTS = 2
Z, Y, C = 8, 4, 2
X, H = 4, 2
F32, BF16 = jnp.float32, jnp.bfloat16
NT = (((1,), (1,)), ((), ()))


def place(z, y, core):
    return (z * Y + y) * C + core


def every(order):
    return [order(z, y, core) for z in range(Z) for y in range(Y) for core in range(C)]


def flipped(bits):
    return every(lambda z, y, core: (place(z, y, core), place(z ^ (bits // Y), y ^ (bits % Y), core)))


OTHER_CORE = every(lambda z, y, core: (place(z, y, core), place(z, y, 1 - core)))
Z_STEPS = (16, 8, 4)
Y_STEPS = ((1, 3), (3, 1))
X_RINGS = [[x * H + h for x in range(X)] for h in range(H)]


def corner(far_h, far_core):
    return [(i, i ^ (far_core * X * H + far_h)) for i in range(Z * Y * C * X * H)]


def after(value, *earlier):
    for e in earlier:
        value = value + jnp.minimum(jnp.abs(e[(0,) * e.ndim]), 0).astype(value.dtype)
    return value


def params(**more):
    return pltpu.CompilerParams(vmem_limit_bytes=50 * 1024 * 1024, **more)


def cost(flops, moved):
    return pl.CostEstimate(flops=flops, bytes_accessed=moved, transcendentals=0)


def regroup(width, parts, half):
    rows = half // parts
    column = lax.broadcasted_iota(jnp.int32, (1, width), 1)
    block, inside = column // (2 * half), column % (2 * half)
    side, deep = inside // half, inside % half
    part, row = deep // rows, deep % rows
    blocks = width // (2 * half)
    source = ((side * parts + part) * blocks + block) * rows + row
    here = lax.broadcasted_iota(jnp.int32, (width, width), 0)
    return jnp.where(here == source, 1.0, 0.0).astype(BF16)


def split_kernel(parts, half, who, x_ref, p_ref, keep_ref, send_ref, proj_ref, order):
    core = who[0]
    width = order.shape[0]
    piece = width // (2 * parts)
    full = keep_ref.shape[1] // parts
    order[...] = regroup(width, parts, half)
    groups = x_ref.shape[1] // width

    def mix(ref):
        stacked = jnp.concatenate([ref[:, g * width : (g + 1) * width] for g in range(groups)], axis=0)
        return lax.dot_general(stacked, order[...], NT, preferred_element_type=F32).astype(BF16)

    x_mixed, p_mixed = mix(x_ref), mix(p_ref)

    def deal(mixed, ref, side):
        rows = ref.shape[0]
        for g in range(groups):
            for p in range(parts):
                to = slice(p * full + g * piece, p * full + (g + 1) * piece)
                at = (side * parts + p) * piece
                ref[:, to] = mixed[g * rows : (g + 1) * rows, at : at + piece]

    for value in range(C):

        @pl.when(core == value)
        def _(value=value):
            deal(x_mixed, keep_ref, value)
            deal(x_mixed, send_ref, 1 - value)
            deal(p_mixed, proj_ref, value)


def compress_kernel(xk_ref, xr_ref, gk_ref, gr_ref, proj_ref, mask_ref, out_ref, masked):
    rank = proj_ref.shape[0]
    pairs = mask_ref.shape[0]
    side = 2 * mask_ref.shape[0]
    block = gk_ref.shape[1] // side
    for j in range(pairs):
        masked[j * rank : (j + 1) * rank, :] = proj_ref[...] * mask_ref[j : j + 1, :]
    masked[pairs * rank : (pairs + 1) * rank, :] = proj_ref[...]
    held = []
    for x_ref in (xk_ref, xr_ref):
        held.append(lax.dot_general(masked[...], x_ref[...], NT, preferred_element_type=F32))
    for panel in range(side):
        total = None
        for seen, g_ref in zip(held, (gk_ref, gr_ref)):
            j = panel // 2
            part = seen[j * rank : (j + 1) * rank, :]
            if panel % 2:
                part = seen[pairs * rank :, :] - part
            high = part.astype(BF16)
            low = (part - high.astype(F32)).astype(BF16)
            grads = g_ref[:, panel * block : (panel + 1) * block]
            term = jnp.dot(high, grads, preferred_element_type=F32) + jnp.dot(low, grads, preferred_element_type=F32)
            total = term if total is None else total + term
        out_ref[:, panel, :] = total


def main_kernel(first, last, who, rows_ref, *rest):
    rest = list(rest)
    chunks = [rest.pop(0) for _ in range(4 if first else 1)]
    xk_ref, xr_ref, gk_ref, gr_ref = (rest.pop(0) for _ in range(4))
    acc_k, acc_r = (None, None) if first else (rest.pop(0), rest.pop(0))
    grad_ref, hk_ref, hr_ref, dense = rest
    core, mine = who[0], who[1]
    deep, block = chunks[0].shape[-2:]
    panels = rows_ref.shape[0]
    some = panels // 2
    tokens = xk_ref.shape[0]
    blank = jnp.zeros((deep, block), BF16)

    def lay(panel, slot, weights):
        at = pl.multiple_of(rows_ref[panel, slot] * deep, deep)
        other = panel ^ 1
        dense[pl.ds(at, deep), panel * block : (panel + 1) * block] = weights
        dense[pl.ds(at, deep), other * block : (other + 1) * block] = blank

    def put(slot, carry):
        for panel in range(panels):
            lay(panel, slot, chunks[0][panel, slot, core])
        return carry

    def put_steps(i, carry):
        for q, (y_first, y_second) in enumerate(Y_STEPS):
            for late in range(2):
                far = (i // 8) * y_first ^ late * y_second
                slot = mine ^ far ^ ((i // 4) % 2 * Z_STEPS[2]) ^ ((i // 2) % 2 * Z_STEPS[1]) ^ (i % 2 * Z_STEPS[0])
                for n in range(some):
                    lay(q * some + n, slot, chunks[2 * q + late][i, n])
        return carry

    if first:
        lax.fori_loop(0, chunks[0].shape[0], put_steps, 0)
    else:
        lax.fori_loop(0, chunks[0].shape[1], put, 0)
    share = dense.shape[0] // (X * H)
    for x in range(X):
        tile = dense[x * H * share : (x + 1) * H * share, :]
        for t, g_ref in enumerate((gk_ref, gr_ref)):
            out = lax.dot_general(g_ref[...], tile, NT, preferred_element_type=F32).astype(BF16)
            for h in range(H):
                grad_ref[x, h, t * tokens : (t + 1) * tokens, :] = out[:, h * share : (h + 1) * share]
    step = 2 * block
    for n in range(panels // 2):
        cols = slice(n * step, (n + 1) * step)
        for x_ref, h_ref, acc in ((xk_ref, hk_ref, acc_k), (xr_ref, hr_ref, acc_r)):
            out = jnp.dot(x_ref[...], dense[:, cols], preferred_element_type=F32)
            if acc is not None:
                out = out + acc[:, cols]
            h_ref[:, cols] = out.astype(h_ref.dtype)


def reduce_kernel(parts, who, *refs):
    crossings, outs = refs[:parts], refs[parts:]
    h_here = who[2]
    tokens = outs[0].shape[1]
    for far_h in range(H):
        for side in range(C):
            at = pl.ds(side * tokens, tokens)
            for p, r_ref in enumerate(crossings):
                total = r_ref[0, h_here ^ far_h, at, :].astype(F32)
                for x in range(1, X):
                    total = total + r_ref[x, h_here ^ far_h, at, :].astype(F32)
                outs[far_h * C + side][p] = total.astype(BF16)


def final_kernel(parts, half, who, *refs):
    near, out_ref = refs[:4], refs[4]
    width = out_ref.shape[1]
    columns = []
    for side in range(C):
        for p in range(parts):
            mine = near[0][p].astype(F32) + near[2][p].astype(F32)
            other = near[1][p].astype(F32) + near[3][p].astype(F32)
            columns.append(jnp.where(who[0] == side, mine, other).astype(BF16))
    piece = 128
    group = 2 * parts * piece
    order = regroup(group, parts, half)
    for g in range(width // group):
        together = jnp.concatenate([c[:, g * piece : (g + 1) * piece] for c in columns], axis=1)
        out_ref[:, g * group : (g + 1) * group] = jnp.dot(together, order, preferred_element_type=F32).astype(BF16)


def body(inputs, weight_blocks, block_rows, grad_hidden, projection, momentum):
    tokens, width = inputs.shape
    panels, half, block = weight_blocks.shape
    slots = block_rows.shape[1]
    rank = projection.shape[0]
    row_blocks = width // block
    parts, deep = PARTS, half // PARTS
    units = grad_hidden.shape[1]
    here = lax.axis_index("dp")
    who = jnp.stack([here % C, here // C, lax.axis_index("tensor") % H]).astype(jnp.int32)
    smem = pl.BlockSpec(memory_space=pltpu.SMEM)
    vmem = pl.BlockSpec(memory_space=pltpu.VMEM)
    sds = jax.ShapeDtypeStruct

    keep, send, proj = pl.pallas_call(
        functools.partial(split_kernel, parts, half),
        out_shape=(sds((tokens, width // 2), BF16), sds((tokens, width // 2), BF16), sds((rank, width // 2), BF16)),
        in_specs=[smem, vmem, vmem],
        out_specs=(vmem, vmem, vmem),
        scratch_shapes=[pltpu.VMEM((2 * parts * block, 2 * parts * block), BF16)],
        compiler_params=params(),
        cost_estimate=cost(4 * 10**9, 6 * 10**6),
        name="split",
    )(who, inputs, projection)
    received = lax.ppermute(send, "dp", OTHER_CORE)
    grads_received = lax.ppermute(grad_hidden, "dp", OTHER_CORE)

    named = (block_rows[0::2, :, None] == jnp.arange(row_blocks, dtype=jnp.int32)).any(axis=1)
    mask = jnp.tile(jnp.repeat(named, deep, axis=1), (1, parts)).astype(BF16)
    def compress(first_seen, second_seen):
        out = pl.pallas_call(
            compress_kernel,
            out_shape=sds((rank, panels, block), F32),
            in_specs=[vmem] * 6,
            out_specs=vmem,
            scratch_shapes=[pltpu.VMEM(((panels // 2 + 1) * rank, width // 2), BF16)],
            compiler_params=params(),
            cost_estimate=cost(4 * 10**9, 6 * 10**6),
            name="compress",
        )(keep, received, grad_hidden, grads_received, proj, after(mask, first_seen))
        return out, lax.all_to_all(after(out, second_seen), "dp", 0, 0, tiled=True).sum(axis=0)

    crossings, acc = [], ()
    whole = lambda *shape: pl.BlockSpec(shape, lambda i: (0,) * len(shape))
    for p in range(parts):
        own = weight_blocks[:, p * deep : (p + 1) * deep]
        if p == 0:
            chunks, seen = own[None], []
            for step in Z_STEPS:
                if step == Z_STEPS[2]:
                    compressed, summed = compress(*seen)
                    chunks = after(chunks, compressed)
                far = lax.ppermute(chunks, "dp", flipped(step))
                seen.append(far)
                chunks = jnp.concatenate([chunks, far])
            gathered = []
            for q, (y_first, y_second) in enumerate(Y_STEPS):
                some = chunks[:, q * (panels // 2) : (q + 1) * (panels // 2)]
                some = jnp.concatenate([some, lax.ppermute(some, "dp", flipped(y_first))])
                gathered += [some, lax.ppermute(some, "dp", flipped(y_second))]
            shapes = [whole(16, panels // 2, deep, block)] * 4
        else:
            gathered = [lax.all_gather(own, "dp", axis=1, tiled=True).reshape(panels, slots, C, deep, block)]
            shapes = [whole(panels, slots, C, deep, block)]
        turn = after(who, crossed) if p else after(who, summed)
        first, last = p == 0, p == parts - 1
        part_spec = pl.BlockSpec((tokens, row_blocks * deep), lambda i, p=p: (0, p))
        h_types = (F32, BF16 if last else F32)
        share = 8 * deep
        grad, *acc = pl.pallas_call(
            functools.partial(main_kernel, first, last),
            grid=(1,),
            out_shape=(
                sds((X, H, 2 * tokens, share), BF16),
                sds((tokens, units), h_types[0]),
                sds((tokens, units), h_types[1]),
            ),
            in_specs=[smem, smem, *shapes, part_spec, part_spec]
            + [whole(tokens, units)] * (2 if first else 4),
            out_specs=(whole(X, H, 2 * tokens, share), whole(tokens, units), whole(tokens, units)),
            scratch_shapes=[pltpu.VMEM((row_blocks * deep, units), BF16)],
            compiler_params=params(),
            cost_estimate=cost(8 * 10**9 // parts, 8 * 10**6),
            name="main",
        )(turn, block_rows, *gathered, keep, received, grad_hidden, grads_received, *acc)
        crossed = lax.all_to_all(grad, "tensor", 0, 0, tiled=True, axis_index_groups=X_RINGS)
        crossings.append(crossed)
    out = pl.pallas_call(
        functools.partial(reduce_kernel, parts),
        out_shape=(sds((parts, tokens, share), BF16),) * 4,
        in_specs=[smem] + [vmem] * parts,
        out_specs=(vmem,) * 4,
        compiler_params=params(),
        cost_estimate=cost(10**6, 10**6),
        name="reduce",
    )(who, *crossings)
    finals = [out[0]] + [lax.ppermute(out[i], ("dp", "tensor"), corner(i // C, i % C)) for i in range(1, 4)]
    hidden_received = lax.ppermute(acc[1], "dp", OTHER_CORE)
    hidden = (acc[0] + hidden_received.astype(F32)).astype(BF16)
    new_momentum = 0.9 * momentum + summed.reshape(1, units)
    input_grad = pl.pallas_call(
        functools.partial(final_kernel, parts, half),
        out_shape=sds((tokens, width // (X * H)), BF16),
        in_specs=[smem] + [vmem] * 4,
        out_specs=vmem,
        compiler_params=params(),
        cost_estimate=cost(10**8, 10**6),
        name="final",
    )(who, *finals)
    return hidden, input_grad, new_momentum


def solution(mesh):
    placed = (
        P("dp", None),
        P("tensor", "dp", None),
        P("tensor", None),
        P("dp", "tensor"),
        P(),
        P("dp", "tensor"),
    )
    return jax.shard_map(
        body,
        mesh=mesh,
        in_specs=placed,
        out_specs=(P("dp", "tensor"), P("dp", "tensor"), P("dp", "tensor")),
        check_vma=False,
    )
```
